512 devices in a mesh: seq: 64 (over z, y_lo, core), head: 8 (over x, y_hi).
Axes of the slice: x: 4, y: 8 (y_hi: 2, y_lo: 4; y = y_hi * 4 + y_lo), z: 8, core: 2. Of those that a mesh axis runs over, the one named last changes fastest.
Arguments:
- queries: bfloat16 [2, 1024, 16384], P(None, 'seq', 'head'), may hold values from -80 to 80
- prefix_keys: bfloat16 [16384, 1024], P(('seq', 'head')), may hold values from -4 to 4
- prefix_values: bfloat16 [16384, 1024], P(('seq', 'head')), may hold values from -6 to 6
- cache_keys: bfloat16 [1024, 2, 1024], P('seq', None, 'head'), may hold values from -6 to 6
- cache_values: bfloat16 [1024, 2, 1024], P('seq', None, 'head'), may hold values from -6 to 6
- new_keys: bfloat16 [2, 1024, 1024], P(None, 'seq', 'head'), may hold values from -6 to 6
- new_values: bfloat16 [2, 1024, 1024], P(None, 'seq', 'head'), may hold values from -6 to 6
- suffix_len: int32 [1024], P('seq'), may hold values from 0 to 2
- out_weight: bfloat16 [16384, 16384], P('head', 'seq'), may hold values from -0.046875 to 0.046875
Outputs:
- projected: bfloat16 [2, 1024, 16384], P(None, 'head', 'seq')
The draws below stay inside these ranges and needn't reach their ends.
Inputs may be any that keep to these rules, and one draw needn't show every extreme that they name: `suffix_len`: number of earlier suffix tokens of each completion; cache slots from it on are unused.
All inputs are finite; a program needn't handle non-finite values.
Results may differ from the reference program's by a relative error of at most 0.019.
Values may be sent and summed in bfloat16 or wider, within the bound.
No kernel may reach another device: no remote copies, remote signals or barrier semaphores. Data moves between devices by JAX's collectives and lax.ppermute only.
A program may use at most 64 MiB of HBM per device.

```python
import jax
import jax.numpy as jnp
from jax import lax

D = 16384
QH = 128
KVH = 8
HD = 128
SUF = 2
B = 1024
P_SIZE = 16384


def base_keys(key):
    return jnp.clip(jax.random.normal(key, (P_SIZE, KVH * HD), jnp.float32), -4.0, 4.0)


def draw_prefix_keys(key, part):
    base = base_keys(key)
    return base.astype(jnp.bfloat16)


def draw_queries(key, part):
    key = jax.random.fold_in(key, 23)
    draws = jnp.clip(2.5 * jax.random.normal(key, (2, B, QH * HD), jnp.float32), -10.0, 10.0)
    return draws.astype(jnp.bfloat16)


def place_ends(values, stream_key, smallest, high):
    extent = values.shape
    place = [jax.random.randint(jax.random.fold_in(stream_key, axis), (), 0, extent[axis]) for axis in range(len(extent))]
    values = values.at[tuple(place)].set(smallest)
    longest = extent.index(max(extent))
    place[longest] = (place[longest] + 1) % extent[longest]
    return values.at[tuple(place)].set(high)


def block_levels(key, dims, pieces, smallest, top_value):
    gain = 1.0
    for dim, blocks in pieces:
        steps = jax.random.uniform(jax.random.fold_in(jax.random.fold_in(key, 6), dim), (blocks,), jnp.float32, smallest / len(pieces), top_value / len(pieces))
        gain = gain * jnp.repeat(jnp.exp(steps), dims[dim] // blocks).reshape((-1,) + (1,) * (len(dims) - 1 - dim))
    return gain


def scatter_about(stream_key, dims, scale, reach, shards=(), held_as=jnp.bfloat16):
    values = scale * jax.random.normal(stream_key, dims, jnp.float32)
    if shards:
        values = values * block_levels(stream_key, dims, shards, -0.22, 0.18)
    return jnp.clip(values, -reach, reach).astype(held_as)


def setup_inputs(seed: int = 0) -> dict:
    keys = jax.random.split(jax.random.key(seed), 10)
    return {
        "queries": draw_queries(jax.random.fold_in(keys[9], 71), 0),
        "prefix_keys": draw_prefix_keys(jax.random.fold_in(keys[9], 71), 0),
        "prefix_values": scatter_about(keys[2], (P_SIZE, KVH * HD), 1.0, 6.0, ((0, 512),)),
        "cache_keys": scatter_about(keys[3], (B, SUF, KVH * HD), 1.0, 6.0, ((0, 64), (2, 8))),
        "cache_values": scatter_about(keys[4], (B, SUF, KVH * HD), 1.0, 6.0, ((0, 64), (2, 8))),
        "new_keys": scatter_about(keys[5], (2, B, KVH * HD), 1.0, 6.0, ((1, 64), (2, 8))),
        "new_values": scatter_about(keys[6], (2, B, KVH * HD), 1.0, 6.0, ((1, 64), (2, 8))),
        "suffix_len": place_ends(jax.random.randint(keys[7], (B,), 0, SUF + 1), jax.random.fold_in(keys[7], 1), 0, SUF).astype(jnp.int32),
        "out_weight": scatter_about(keys[8], (QH * HD, D), (QH * HD) ** -0.5, 0.046875, ((0, 8), (1, 64))),
    }


def reference(queries, prefix_keys, prefix_values, cache_keys, cache_values, new_keys, new_values, suffix_len, out_weight):
    group_size = QH // KVH
    score_scale = HD ** -0.5
    prompt_keys = prefix_keys.reshape(P_SIZE, KVH, HD).transpose(1, 0, 2)
    prompt_values = prefix_values.reshape(P_SIZE, KVH, HD).transpose(1, 0, 2)
    results = []
    for step in range(2):
        step_queries = queries[step].reshape(B, KVH, group_size, HD).transpose(1, 0, 2, 3)
        fresh_keys = jnp.swapaxes(new_keys[: step + 1], 0, 1).reshape(B, step + 1, KVH, HD)
        fresh_values = jnp.swapaxes(new_values[: step + 1], 0, 1).reshape(B, step + 1, KVH, HD)
        suffix_keys = jnp.concatenate([cache_keys.reshape(B, SUF, KVH, HD), fresh_keys], axis=1).transpose(2, 0, 1, 3)
        suffix_values = jnp.concatenate([cache_values.reshape(B, SUF, KVH, HD), fresh_values], axis=1).transpose(2, 0, 1, 3)
        slots = jnp.arange(SUF + step + 1, dtype=jnp.int32)
        valid = (slots[None, :] < suffix_len[:, None]) | (slots[None, :] >= SUF)

        def one_head(items):
            head_queries, head_keys, head_values, tail_keys, tail_values = items
            qf = head_queries.astype(jnp.float32)
            prompt_scores = jnp.einsum('bgd,pd->bgp', qf, head_keys.astype(jnp.float32)) * score_scale
            tail_scores = jnp.einsum('bgd,bjd->bgj', qf, tail_keys.astype(jnp.float32)) * score_scale
            tail_scores = jnp.where(valid[:, None, :], tail_scores, jnp.float32(-1e30))
            row_max = jnp.maximum(jnp.max(prompt_scores, axis=-1), jnp.max(tail_scores, axis=-1))
            prompt_weights = jnp.exp(prompt_scores - row_max[..., None])
            tail_weights = jnp.where(valid[:, None, :], jnp.exp(tail_scores - row_max[..., None]), jnp.float32(0.0))
            total = jnp.sum(prompt_weights, axis=-1) + jnp.sum(tail_weights, axis=-1)
            prompt_rounded = lax.optimization_barrier(prompt_weights.astype(jnp.bfloat16)).astype(jnp.float32)
            tail_rounded = lax.optimization_barrier(tail_weights.astype(jnp.bfloat16)).astype(jnp.float32)
            weighted = jnp.einsum('bgp,pd->bgd', prompt_rounded, head_values.astype(jnp.float32))
            weighted = weighted + jnp.einsum('bgj,bjd->bgd', tail_rounded, tail_values.astype(jnp.float32))
            return (weighted / total[..., None]).astype(jnp.bfloat16)

        heads = lax.map(one_head, (step_queries, prompt_keys, prompt_values, suffix_keys, suffix_values))
        attended = heads.transpose(1, 0, 2, 3).reshape(B, QH * HD)
        results.append(jnp.dot(attended, out_weight, preferred_element_type=jnp.float32).astype(jnp.bfloat16))
    return jnp.stack(results, axis=0)
```

```python
import functools
import math

import jax
import jax.numpy as jnp
from jax import lax
from jax.experimental import pallas as pl
from jax.experimental.pallas import tpu as pltpu
from jax.sharding import Mesh
from jax.sharding import PartitionSpec as P

HD = 128
SUF = 2
HEADS = 16
LOG2_SCALE = HD ** -0.5 * math.log2(math.e)
Y = ("u", "v")
HEAD = ("x", "w")
SEQ = ("z", "u", "v", "c")
VMEM_BYTES = 48 * 1024 * 1024


def shift(size, step):
    return [(index, (index + step) % size) for index in range(size)]


def attention_kernel(q_ref, own_ref, other_ref, out_ref):
    rows = q_ref.shape[0]
    sources = own_ref.shape[0]
    half = own_ref.shape[1] // 2
    keys = []
    values = []
    for ref in (own_ref, other_ref):
        for part in range(2):
            span = slice(part * sources // 2, (part + 1) * sources // 2)
            keys.append(ref[span, :half, :].reshape(-1, HD))
            block = ref[span, half:, :].reshape(-1, HD)
            values.append(jnp.concatenate([block, jnp.ones_like(block)], axis=1))
    lane = lax.broadcasted_iota(jnp.int32, (rows, HD), 1)
    pieces = jnp.zeros((rows, HD), jnp.float32)
    per_tile = HEADS // 2
    for tile in range(2):
        q = jnp.concatenate(
            [q_ref[:, (tile * per_tile + g) * HD : (tile * per_tile + g + 1) * HD] for g in range(per_tile)],
            axis=0,
        )
        scores = [
            lax.dot_general(q, k, (((1,), (1,)), ((), ())), preferred_element_type=jnp.float32)
            for k in keys
        ]
        top = scores[0].max(axis=1, keepdims=True)
        for s in scores[1:]:
            top = jnp.maximum(top, s.max(axis=1, keepdims=True))
        acc = None
        for s, v in zip(scores, values):
            p = jnp.exp2((s - top) * LOG2_SCALE).astype(jnp.bfloat16)
            term = jnp.dot(p, v, preferred_element_type=jnp.float32)
            acc = term if acc is None else acc + term
        total = acc[:, HD : HD + 1]
        mean = acc[:, :HD] / total
        level = top * LOG2_SCALE + jnp.log2(total)
        first = level.astype(jnp.bfloat16).astype(jnp.float32)
        rest = level - first
        second = rest.astype(jnp.bfloat16).astype(jnp.float32)
        third = rest - second
        for g in range(per_tile):
            head = tile * per_tile + g
            span = slice(g * rows, (g + 1) * rows)
            out_ref[:, head * HD : (head + 1) * HD] = mean[span].astype(jnp.bfloat16)
            for place, piece in enumerate((first, second, third)):
                pieces = jnp.where(lane == place * HEADS + head, piece[span], pieces)
    out_ref[:, HEADS * HD :] = pieces.astype(jnp.bfloat16)


def attend(q, own, other):
    rows = q.shape[0]
    return pl.pallas_call(
        attention_kernel,
        out_shape=jax.ShapeDtypeStruct((rows, HEADS * HD + HD), jnp.bfloat16),
        compiler_params=pltpu.CompilerParams(vmem_limit_bytes=VMEM_BYTES),
        name="attend",
    )(q, own, other)


def combine_kernel(q_ref, k_ref, v_ref, len_ref, m0_ref, m1_ref, m2_ref, m3_ref, out_ref):
    rows = q_ref.shape[0]
    local = rows // 2
    width = HEADS * HD
    parts = (m0_ref, m1_ref, m2_ref, m3_ref)
    lane = lax.broadcasted_iota(jnp.int32, (rows, HD), 1)
    step_one = lax.broadcasted_iota(jnp.int32, (rows, 1), 0) >= local
    used = jnp.concatenate([len_ref[...], len_ref[...]], axis=0)
    valid = (used > 0, used > 1, used >= 0, step_one)
    suffix_values = []
    logits = []
    for j in range(4):
        key = jnp.concatenate([k_ref[j], k_ref[j]], axis=0)
        suffix_values.append(jnp.concatenate([v_ref[j], v_ref[j]], axis=0))
        row = jnp.full((rows, HD), -1e30, jnp.float32)
        for g in range(HEADS):
            q = q_ref[:, g * HD : (g + 1) * HD].astype(jnp.float32)
            dot = jnp.sum(q * key, axis=1, keepdims=True) * LOG2_SCALE
            row = jnp.where(lane == g, dot, row)
        logits.append(jnp.where(valid[j], row, jnp.float32(-1e30)))
    levels = []
    for ref in parts:
        tail = ref[:, width:].astype(jnp.float32)
        level = tail + pltpu.roll(tail, HD - HEADS, 1) + pltpu.roll(tail, HD - 2 * HEADS, 1)
        levels.append(level)
    top = functools.reduce(jnp.maximum, levels + logits)
    factors = [jnp.exp2(level - top) for level in levels]
    weights = [
        jnp.where(valid[j], jnp.exp2(logits[j] - top), jnp.float32(0.0)) for j in range(4)
    ]
    total = functools.reduce(jnp.add, factors + weights)
    scale = 1.0 / total
    factors = [f * scale for f in factors]
    weights = [w * scale for w in weights]
    for g in range(HEADS):
        cols = slice(g * HD, (g + 1) * HD)
        acc = jnp.zeros((rows, HD), jnp.float32)
        for ref, f in zip(parts, factors):
            acc = acc + f[:, g : g + 1] * ref[:, cols].astype(jnp.float32)
        for j in range(4):
            acc = acc + weights[j][:, g : g + 1] * suffix_values[j]
        out_ref[:, cols] = acc.astype(jnp.bfloat16)


def combine(q, keys, values, lens, parts):
    return pl.pallas_call(
        combine_kernel,
        out_shape=jax.ShapeDtypeStruct(q.shape, jnp.bfloat16),
        compiler_params=pltpu.CompilerParams(vmem_limit_bytes=VMEM_BYTES),
        name="combine",
    )(q, keys, values, lens, *parts)


def project_kernel(place_ref, *refs):
    blocks = refs[:8]
    own_ref, other_ref, out_ref, held = refs[8:]
    rows = blocks[0].shape[0]

    @pl.when(pl.program_id(0) == 0)
    def _():
        for index, block in enumerate(blocks):
            held[index * rows : (index + 1) * rows, :] = block[...]

    first = place_ref[0]
    core = place_ref[1]
    for ref, side in ((own_ref, core), (other_ref, 1 - core)):
        terms = jnp.dot(held[...], ref[0], preferred_element_type=jnp.float32).astype(jnp.bfloat16)
        for index in range(8):
            where = lax.rem(first + index, 8)
            out_ref[0, side, where] = terms[index * rows : (index + 1) * rows]


def project(place, blocks, own, other):
    rows, depth = blocks[0].shape
    quarters, _, cols = own.shape
    whole = pl.BlockSpec((rows, depth), lambda i, place: (0, 0))
    part = pl.BlockSpec((1, depth, cols), lambda i, place: (i, 0, 0))
    return pl.pallas_call(
        project_kernel,
        out_shape=jax.ShapeDtypeStruct((quarters, 2, 8, rows, cols), jnp.bfloat16),
        grid_spec=pltpu.PrefetchScalarGridSpec(
            num_scalar_prefetch=1,
            grid=(quarters,),
            in_specs=[whole] * 8 + [part, part],
            out_specs=pl.BlockSpec((1, 2, 8, rows, cols), lambda i, place: (i, 0, 0, 0, 0)),
            scratch_shapes=[pltpu.VMEM((8 * rows, depth), jnp.bfloat16)],
        ),
        compiler_params=pltpu.CompilerParams(vmem_limit_bytes=VMEM_BYTES),
        name="project",
    )(place, *blocks, own, other)


def per_device(
    queries,
    prefix_keys,
    prefix_values,
    cache_keys,
    cache_values,
    new_keys,
    new_values,
    suffix_len,
    out_weight,
):
    local = queries.shape[1]
    count = prefix_keys.shape[0]
    q = queries.reshape(2 * local, HEADS * HD)

    weight_y = lax.all_gather(out_weight, Y, axis=0, tiled=False)

    q_parts = [q] + [lax.ppermute(q, Y, shift(4, k)) for k in (1, 2, 3)]

    split = [
        jnp.swapaxes(rows.reshape(count, 8, HD), 0, 1) for rows in (prefix_keys, prefix_values)
    ]
    sent = jnp.concatenate(split, axis=1)
    sent = jnp.broadcast_to(sent[None], (8,) + sent.shape).reshape(64, 2 * count, HD)
    own = lax.all_to_all(sent, ("z",) + HEAD, 0, 0, tiled=True)
    other = lax.ppermute(own, "c", shift(2, 1))

    parts = [None] * 4
    for k in (2, 1, 3, 0):
        message = attend(q_parts[k], own, other)
        parts[k] = message if k == 0 else lax.ppermute(message, Y, shift(4, -k))

    suffix_keys = jnp.stack(
        [cache_keys[:, 0], cache_keys[:, 1], new_keys[0], new_keys[1]], axis=0
    ).astype(jnp.float32)
    suffix_values = jnp.stack(
        [cache_values[:, 0], cache_values[:, 1], new_values[0], new_values[1]], axis=0
    ).astype(jnp.float32)
    attended = combine(q, suffix_keys, suffix_values, suffix_len.reshape(local, 1), parts)

    blocks = {0: attended}
    up = attended
    down = attended
    for step in range(1, 5):
        up = lax.ppermute(up, "z", shift(8, 1))
        blocks[-step] = up
        if step < 4:
            down = lax.ppermute(down, "z", shift(8, -1))
            blocks[step] = down
    weight_other = lax.ppermute(weight_y, "c", shift(2, 1))
    place = jnp.stack([lax.rem(lax.axis_index("z") + 4, 8), lax.axis_index("c")]).astype(jnp.int32)
    terms = project(place, [blocks[offset] for offset in range(-4, 4)], weight_y, weight_other)

    rows, cols = terms.shape[3:]
    arrived = lax.all_to_all(
        terms.reshape(64, rows, cols), Y + ("c",) + HEAD, 0, 0, tiled=True
    ).reshape(8, 8, 2, local, cols)
    summed = jnp.sum(arrived.astype(jnp.float32), axis=1).astype(jnp.bfloat16)
    return jnp.swapaxes(summed, 0, 1).reshape(2, 8 * local, cols)


def solution(mesh):
    split_mesh = Mesh(mesh.devices.reshape(8, 2, 2, 2, 4, 2), SEQ + HEAD)
    in_specs = (
        P(None, SEQ, HEAD),
        P(SEQ + HEAD, None),
        P(SEQ + HEAD, None),
        P(SEQ, None, HEAD),
        P(SEQ, None, HEAD),
        P(None, SEQ, HEAD),
        P(None, SEQ, HEAD),
        P(SEQ),
        P(HEAD, SEQ),
    )
    out_specs = P(None, HEAD, SEQ)
    return jax.shard_map(
        per_device, mesh=split_mesh, in_specs=in_specs, out_specs=out_specs, check_vma=False
    )
```

```python
import functools
import math

import jax
import jax.numpy as jnp
from jax import lax
from jax.experimental import pallas as pl
from jax.experimental.pallas import tpu as pltpu
from jax.sharding import Mesh
from jax.sharding import PartitionSpec as P

HD = 128
SUF = 2
HEADS = 16
LOG2_SCALE = HD ** -0.5 * math.log2(math.e)
Y = ("u", "v")
HEAD = ("x", "w")
SEQ = ("z", "u", "v", "c")
CHUNK = 8
EARLY = 1280
VMEM_BYTES = 48 * 1024 * 1024


def shift(size, step):
    return [(index, (index + step) % size) for index in range(size)]


def partner(size, bits):
    return [(index, index ^ bits) for index in range(size)]


def ring(value):
    blocks = {0: value}
    up = value
    down = value
    for step in range(1, 5):
        up = lax.ppermute(up, "z", shift(8, 1))
        blocks[-step] = up
        if step < 4:
            down = lax.ppermute(down, "z", shift(8, -1))
            blocks[step] = down
        yield blocks


def swap(value):
    return lax.ppermute(value, "c", partner(2, 1))


def after(value, *others, space=pl.ANY):
    def nothing(*refs):
        pass

    return pl.pallas_call(
        nothing,
        out_shape=jax.ShapeDtypeStruct(value.shape, value.dtype),
        in_specs=[pl.BlockSpec(memory_space=space)] + [pl.BlockSpec(memory_space=pl.ANY)] * len(others),
        out_specs=pl.BlockSpec(memory_space=space),
        input_output_aliases={0: 0},
        name="after",
    )(value, *others)


def attention_kernel(q_ref, *refs):
    out_ref = refs[-1]
    rows = q_ref.shape[0]
    half = refs[0].shape[1] // 2
    q = jnp.concatenate([q_ref[:, g * HD : (g + 1) * HD] for g in range(HEADS)], axis=0)
    top = None
    acc = None
    for ref in refs[:-1]:
        for start in range(0, ref.shape[0], CHUNK):
            span = slice(start, start + CHUNK)
            keys = ref[span, :half, :].reshape(-1, HD)
            block = ref[span, half:, :].reshape(-1, HD)
            values = jnp.concatenate([block, jnp.ones_like(block)], axis=1)
            scores = lax.dot_general(
                q, keys, (((1,), (1,)), ((), ())), preferred_element_type=jnp.float32
            )
            highest = scores.max(axis=1, keepdims=True)
            if top is not None:
                highest = jnp.maximum(top, highest)
            weights = jnp.exp2((scores - highest) * LOG2_SCALE).astype(jnp.bfloat16)
            term = jnp.dot(weights, values, preferred_element_type=jnp.float32)
            acc = term if acc is None else acc * jnp.exp2((top - highest) * LOG2_SCALE) + term
            top = highest
    total = acc[:, HD : HD + 1]
    mean = acc[:, :HD] / total
    level = top * LOG2_SCALE + jnp.log2(total)
    first = level.astype(jnp.bfloat16).astype(jnp.float32)
    rest = level - first
    second = rest.astype(jnp.bfloat16).astype(jnp.float32)
    third = rest - second
    lane = lax.broadcasted_iota(jnp.int32, (rows, HD), 1)
    pieces = jnp.zeros((rows, HD), jnp.float32)
    for g in range(HEADS):
        span = slice(g * rows, (g + 1) * rows)
        out_ref[:, g * HD : (g + 1) * HD] = mean[span].astype(jnp.bfloat16)
        for place, piece in enumerate((first, second, third)):
            pieces = jnp.where(lane == place * HEADS + g, piece[span], pieces)
    out_ref[:, HEADS * HD :] = pieces.astype(jnp.bfloat16)


def attend(q, blocks):
    rows = q.shape[0]
    return pl.pallas_call(
        attention_kernel,
        out_shape=jax.ShapeDtypeStruct((rows, HEADS * HD + HD), jnp.bfloat16),
        compiler_params=pltpu.CompilerParams(vmem_limit_bytes=VMEM_BYTES),
        name="attend",
    )(q, *blocks)


def combine_kernel(q_ref, k_ref, v_ref, len_ref, m0_ref, m1_ref, m2_ref, m3_ref, out_ref):
    rows = q_ref.shape[0]
    local = rows // 2
    width = HEADS * HD
    parts = (m0_ref, m1_ref, m2_ref, m3_ref)
    lane = lax.broadcasted_iota(jnp.int32, (rows, HD), 1)
    step_one = lax.broadcasted_iota(jnp.int32, (rows, 1), 0) >= local
    used = jnp.concatenate([len_ref[...], len_ref[...]], axis=0)
    valid = (used > 0, used > 1, used >= 0, step_one)
    suffix_values = []
    logits = []
    for j in range(4):
        key = jnp.concatenate([k_ref[j], k_ref[j]], axis=0)
        suffix_values.append(jnp.concatenate([v_ref[j], v_ref[j]], axis=0))
        row = jnp.full((rows, HD), -1e30, jnp.float32)
        for g in range(HEADS):
            q = q_ref[:, g * HD : (g + 1) * HD].astype(jnp.float32)
            dot = jnp.sum(q * key, axis=1, keepdims=True) * LOG2_SCALE
            row = jnp.where(lane == g, dot, row)
        logits.append(jnp.where(valid[j], row, jnp.float32(-1e30)))
    levels = []
    for ref in parts:
        tail = ref[:, width:].astype(jnp.float32)
        level = tail + pltpu.roll(tail, HD - HEADS, 1) + pltpu.roll(tail, HD - 2 * HEADS, 1)
        levels.append(level)
    top = functools.reduce(jnp.maximum, levels + logits)
    factors = [jnp.exp2(level - top) for level in levels]
    weights = [
        jnp.where(valid[j], jnp.exp2(logits[j] - top), jnp.float32(0.0)) for j in range(4)
    ]
    total = functools.reduce(jnp.add, factors + weights)
    scale = 1.0 / total
    factors = [f * scale for f in factors]
    weights = [w * scale for w in weights]
    for g in range(HEADS):
        cols = slice(g * HD, (g + 1) * HD)
        acc = jnp.zeros((rows, HD), jnp.float32)
        for ref, f in zip(parts, factors):
            acc = acc + f[:, g : g + 1] * ref[:, cols].astype(jnp.float32)
        for j in range(4):
            acc = acc + weights[j][:, g : g + 1] * suffix_values[j]
        out_ref[:, cols] = acc.astype(jnp.bfloat16)


def combine(q, keys, values, lens, parts):
    return pl.pallas_call(
        combine_kernel,
        out_shape=jax.ShapeDtypeStruct(q.shape, jnp.bfloat16),
        compiler_params=pltpu.CompilerParams(vmem_limit_bytes=VMEM_BYTES),
        name="combine",
    )(q, keys, values, lens, *parts)


def project_kernel(place_ref, *refs):
    blocks = refs[:-4]
    early_ref, late_ref, out_ref, held = refs[-4:]
    rows = out_ref.shape[3]

    @pl.when(pl.program_id(0) == 0)
    def _():
        start = 0
        for block in blocks:
            held[start : start + block.shape[0], :] = block[...]
            start += block.shape[0]

    first = place_ref[0]
    core = place_ref[1]
    depth = early_ref.shape[1]
    terms = jnp.dot(held[:, :depth], early_ref[0], preferred_element_type=jnp.float32)
    terms += jnp.dot(held[:, depth:], late_ref[0], preferred_element_type=jnp.float32)
    terms = terms.astype(jnp.bfloat16)
    for side in range(2):
        which = core if side == 0 else 1 - core
        for index in range(8):
            where = lax.rem(first + index, 8)
            start = (side * 8 + index) * rows
            out_ref[0, where, which] = terms[start : start + rows]


def project(place, blocks, weights):
    depth = blocks[0].shape[1]
    quarters, _, cols = weights[0].shape
    rows = sum(block.shape[0] for block in blocks) // 16
    whole = [pl.BlockSpec(block.shape, lambda i, place: (0, 0)) for block in blocks]
    return pl.pallas_call(
        project_kernel,
        out_shape=jax.ShapeDtypeStruct((quarters, 8, 2, rows, cols), jnp.bfloat16),
        grid_spec=pltpu.PrefetchScalarGridSpec(
            num_scalar_prefetch=1,
            grid=(quarters,),
            in_specs=whole
            + [pl.BlockSpec((1,) + part.shape[1:], lambda i, place: (i, 0, 0)) for part in weights],
            out_specs=pl.BlockSpec((1, 8, 2, rows, cols), lambda i, place: (i, 0, 0, 0, 0)),
            scratch_shapes=[pltpu.VMEM((16 * rows, depth), jnp.bfloat16)],
        ),
        compiler_params=pltpu.CompilerParams(vmem_limit_bytes=VMEM_BYTES),
        name="project",
    )(place, *blocks, *weights)


def per_device(
    queries,
    prefix_keys,
    prefix_values,
    cache_keys,
    cache_values,
    new_keys,
    new_values,
    suffix_len,
    out_weight,
):
    local = queries.shape[1]
    count = prefix_keys.shape[0]
    q = queries.reshape(2 * local, HEADS * HD)

    early = lax.all_gather(out_weight[:EARLY], Y, axis=0, tiled=False)
    q_parts = [q] + [lax.ppermute(q, Y, partner(4, k)) for k in (1, 2, 3)]

    split = [
        jnp.swapaxes(rows.reshape(count, 8, HD), 0, 1) for rows in (prefix_keys, prefix_values)
    ]
    own = lax.all_to_all(jnp.concatenate(split, axis=1), HEAD, 0, 0, tiled=True)
    held = []
    for step, blocks in enumerate(ring(own), 1):
        if step == 2:
            near = jnp.concatenate([blocks[offset] for offset in (0, -1, 1, -2, 2)], axis=0)
            held += [near, swap(near)]
        if step == 4:
            far = jnp.concatenate([blocks[offset] for offset in (-3, 3, -4)], axis=0)
            held += [far, swap(far)]

    parts = [None] * 4
    for k in (2, 3, 1, 0):
        message = attend(q_parts[k], held)
        parts[k] = message if k == 0 else lax.ppermute(message, Y, partner(4, k))

    suffix_keys = jnp.stack(
        [cache_keys[:, 0], cache_keys[:, 1], new_keys[0], new_keys[1]], axis=0
    ).astype(jnp.float32)
    suffix_values = jnp.stack(
        [cache_values[:, 0], cache_values[:, 1], new_values[0], new_values[1]], axis=0
    ).astype(jnp.float32)
    attended = combine(q, suffix_keys, suffix_values, suffix_len.reshape(local, 1), parts)

    late = lax.all_gather(after(out_weight[EARLY:], attended, early), Y, axis=0, tiled=False)

    for step, blocks in enumerate(ring(attended), 1):
        if step == 3:
            near = swap(jnp.concatenate([blocks[offset] for offset in (-2, -1, 0, 1, 2)], axis=0))
    far = swap(jnp.concatenate([blocks[offset] for offset in (3, -4, -3)], axis=0))
    place = jnp.stack([lax.rem(lax.axis_index("z") + 6, 8), lax.axis_index("c")]).astype(jnp.int32)
    order = (-2, -1, 0, 1, 2, 3, -4, -3)
    terms = project(place, [blocks[offset] for offset in order] + [near, far], [early, late])

    rows, cols = terms.shape[3:]
    arrived = lax.all_to_all(
        terms.reshape(32, 2 * rows, cols), Y + HEAD, 0, 0, tiled=True
    ).reshape(4, 8, 2, 2, local, cols)
    summed = jnp.sum(arrived.astype(jnp.float32), axis=1).astype(jnp.bfloat16)
    return jnp.transpose(summed, (2, 0, 1, 3, 4)).reshape(2, 8 * local, cols)


def solution(mesh):
    split_mesh = Mesh(mesh.devices.reshape(8, 2, 2, 2, 4, 2), SEQ + HEAD)
    in_specs = (
        P(None, SEQ, HEAD),
        P(SEQ + HEAD, None),
        P(SEQ + HEAD, None),
        P(SEQ, None, HEAD),
        P(SEQ, None, HEAD),
        P(None, SEQ, HEAD),
        P(None, SEQ, HEAD),
        P(SEQ),
        P(HEAD, SEQ),
    )
    out_specs = P(None, HEAD, SEQ)
    return jax.shard_map(
        per_device, mesh=split_mesh, in_specs=in_specs, out_specs=out_specs, check_vma=False
    )
```

```python
import functools
import math

import jax
import jax.numpy as jnp
from jax import lax
from jax.experimental import pallas as pl
from jax.experimental.pallas import tpu as pltpu
from jax.sharding import Mesh
from jax.sharding import PartitionSpec as P

HD = 128
SUF = 2
HEADS = 16
LOG2_SCALE = HD ** -0.5 * math.log2(math.e)
Y = ("u", "v")
HEAD = ("x", "w")
SEQ = ("z", "u", "v", "c")
CHUNK = 8
VMEM_BYTES = 48 * 1024 * 1024


def shift(size, step):
    return [(index, (index + step) % size) for index in range(size)]


def partner(size, bits):
    return [(index, index ^ bits) for index in range(size)]


def ring(value):
    blocks = {0: value}
    up = value
    down = value
    for step in range(1, 5):
        up = lax.ppermute(up, "z", shift(8, 1))
        blocks[-step] = up
        if step < 4:
            down = lax.ppermute(down, "z", shift(8, -1))
            blocks[step] = down
        yield blocks


def replicate(value):
    sent = jnp.broadcast_to(value[None], (8,) + value.shape)
    return lax.all_to_all(sent, "z", 0, 0, tiled=True)


def swap(value):
    return lax.ppermute(value, "c", partner(2, 1))


def after(value, *others, space=pl.ANY):
    def nothing(*refs):
        pass

    return pl.pallas_call(
        nothing,
        out_shape=jax.ShapeDtypeStruct(value.shape, value.dtype),
        in_specs=[pl.BlockSpec(memory_space=space)] + [pl.BlockSpec(memory_space=pl.ANY)] * len(others),
        out_specs=pl.BlockSpec(memory_space=space),
        input_output_aliases={0: 0},
        name="after",
    )(value, *others)


def attention_kernel(q_ref, *refs):
    out_ref = refs[-1]
    rows = q_ref.shape[0]
    half = refs[0].shape[1] // 2
    q = jnp.concatenate([q_ref[:, g * HD : (g + 1) * HD] for g in range(HEADS)], axis=0)
    top = None
    acc = None
    for ref in refs[:-1]:
        for start in range(0, ref.shape[0], CHUNK):
            span = slice(start, start + CHUNK)
            keys = ref[span, :half, :].reshape(-1, HD)
            block = ref[span, half:, :].reshape(-1, HD)
            values = jnp.concatenate([block, jnp.ones_like(block)], axis=1)
            scores = lax.dot_general(
                q, keys, (((1,), (1,)), ((), ())), preferred_element_type=jnp.float32
            )
            highest = scores.max(axis=1, keepdims=True)
            if top is not None:
                highest = jnp.maximum(top, highest)
            weights = jnp.exp2((scores - highest) * LOG2_SCALE).astype(jnp.bfloat16)
            term = jnp.dot(weights, values, preferred_element_type=jnp.float32)
            acc = term if acc is None else acc * jnp.exp2((top - highest) * LOG2_SCALE) + term
            top = highest
    total = acc[:, HD : HD + 1]
    mean = acc[:, :HD] / total
    level = top * LOG2_SCALE + jnp.log2(total)
    first = level.astype(jnp.bfloat16).astype(jnp.float32)
    rest = level - first
    second = rest.astype(jnp.bfloat16).astype(jnp.float32)
    third = rest - second
    lane = lax.broadcasted_iota(jnp.int32, (rows, HD), 1)
    pieces = jnp.zeros((rows, HD), jnp.float32)
    for g in range(HEADS):
        span = slice(g * rows, (g + 1) * rows)
        out_ref[:, g * HD : (g + 1) * HD] = mean[span].astype(jnp.bfloat16)
        for place, piece in enumerate((first, second, third)):
            pieces = jnp.where(lane == place * HEADS + g, piece[span], pieces)
    out_ref[:, HEADS * HD :] = pieces.astype(jnp.bfloat16)


def attend(q, blocks):
    rows = q.shape[0]
    return pl.pallas_call(
        attention_kernel,
        out_shape=jax.ShapeDtypeStruct((rows, HEADS * HD + HD), jnp.bfloat16),
        compiler_params=pltpu.CompilerParams(vmem_limit_bytes=VMEM_BYTES),
        name="attend",
    )(q, *blocks)


def combine_kernel(q_ref, k_ref, v_ref, len_ref, m0_ref, m1_ref, m2_ref, m3_ref, out_ref):
    rows = q_ref.shape[0]
    local = rows // 2
    width = HEADS * HD
    parts = (m0_ref, m1_ref, m2_ref, m3_ref)
    lane = lax.broadcasted_iota(jnp.int32, (rows, HD), 1)
    step_one = lax.broadcasted_iota(jnp.int32, (rows, 1), 0) >= local
    used = jnp.concatenate([len_ref[...], len_ref[...]], axis=0)
    valid = (used > 0, used > 1, used >= 0, step_one)
    suffix_values = []
    logits = []
    for j in range(4):
        key = jnp.concatenate([k_ref[j], k_ref[j]], axis=0)
        suffix_values.append(jnp.concatenate([v_ref[j], v_ref[j]], axis=0))
        row = jnp.full((rows, HD), -1e30, jnp.float32)
        for g in range(HEADS):
            q = q_ref[:, g * HD : (g + 1) * HD].astype(jnp.float32)
            dot = jnp.sum(q * key, axis=1, keepdims=True) * LOG2_SCALE
            row = jnp.where(lane == g, dot, row)
        logits.append(jnp.where(valid[j], row, jnp.float32(-1e30)))
    levels = []
    for ref in parts:
        tail = ref[:, width:].astype(jnp.float32)
        level = tail + pltpu.roll(tail, HD - HEADS, 1) + pltpu.roll(tail, HD - 2 * HEADS, 1)
        levels.append(level)
    top = functools.reduce(jnp.maximum, levels + logits)
    factors = [jnp.exp2(level - top) for level in levels]
    weights = [
        jnp.where(valid[j], jnp.exp2(logits[j] - top), jnp.float32(0.0)) for j in range(4)
    ]
    total = functools.reduce(jnp.add, factors + weights)
    scale = 1.0 / total
    factors = [f * scale for f in factors]
    weights = [w * scale for w in weights]
    for g in range(HEADS):
        cols = slice(g * HD, (g + 1) * HD)
        acc = jnp.zeros((rows, HD), jnp.float32)
        for ref, f in zip(parts, factors):
            acc = acc + f[:, g : g + 1] * ref[:, cols].astype(jnp.float32)
        for j in range(4):
            acc = acc + weights[j][:, g : g + 1] * suffix_values[j]
        out_ref[:, cols] = acc.astype(jnp.bfloat16)


def combine(q, keys, values, lens, parts):
    return pl.pallas_call(
        combine_kernel,
        out_shape=jax.ShapeDtypeStruct(q.shape, jnp.bfloat16),
        compiler_params=pltpu.CompilerParams(vmem_limit_bytes=VMEM_BYTES),
        name="combine",
    )(q, keys, values, lens, *parts)


def project_kernel(place_ref, own_ref, other_ref, *refs):
    weights, out_ref = refs[:4], refs[4]
    rows = out_ref.shape[3]
    core, me = place_ref[0], place_ref[1]
    for index, weight in enumerate(weights):
        column = lax.bitwise_xor(me, index)
        for side, rows_ref in enumerate((own_ref, other_ref)):
            terms = jnp.dot(rows_ref[...], weight[...], preferred_element_type=jnp.float32)
            terms = terms.astype(jnp.bfloat16)
            which = lax.bitwise_xor(core, side)
            for z in range(8):
                out_ref[column, z, which] = terms[z * rows : (z + 1) * rows]


def project(place, blocks, weights):
    rows = blocks[0].shape[0] // 8
    cols = weights[0].shape[1]
    whole = list(blocks) + list(weights)
    return pl.pallas_call(
        project_kernel,
        out_shape=jax.ShapeDtypeStruct((4, 8, 2, rows, cols), jnp.bfloat16),
        in_specs=[pl.BlockSpec(memory_space=pltpu.SMEM)]
        + [pl.BlockSpec(memory_space=pltpu.VMEM)] * len(whole),
        compiler_params=pltpu.CompilerParams(vmem_limit_bytes=VMEM_BYTES),
        name="project",
    )(place, *whole)


def per_device(
    queries,
    prefix_keys,
    prefix_values,
    cache_keys,
    cache_values,
    new_keys,
    new_values,
    suffix_len,
    out_weight,
):
    local = queries.shape[1]
    count = prefix_keys.shape[0]
    q = queries.reshape(2 * local, HEADS * HD)

    q_parts = [q] + [lax.ppermute(q, Y, partner(4, k)) for k in (1, 2, 3)]

    split = [
        jnp.swapaxes(rows.reshape(count, 8, HD), 0, 1) for rows in (prefix_keys, prefix_values)
    ]
    own = lax.all_to_all(jnp.concatenate(split, axis=1), HEAD, 0, 0, tiled=True)
    weight_u = lax.ppermute(out_weight, "u", partner(2, 1))
    weight_v = lax.ppermute(out_weight, "v", partner(2, 1))
    held = []
    for step, blocks in enumerate(ring(own), 1):
        if step == 2:
            near = jnp.concatenate([blocks[offset] for offset in (0, -1, 1, -2, 2)], axis=0)
            held += [near, swap(near)]
        if step == 4:
            last = after(blocks[-4], weight_u, weight_v)
            far = jnp.concatenate([blocks[-3], blocks[3], last], axis=0)
            held += [far, swap(far)]

    parts = [None] * 4
    for k in (2, 3, 1, 0):
        message = attend(q_parts[k], held)
        parts[k] = message if k == 0 else lax.ppermute(message, Y, partner(4, k))

    suffix_keys = jnp.stack(
        [cache_keys[:, 0], cache_keys[:, 1], new_keys[0], new_keys[1]], axis=0
    ).astype(jnp.float32)
    suffix_values = jnp.stack(
        [cache_values[:, 0], cache_values[:, 1], new_values[0], new_values[1]], axis=0
    ).astype(jnp.float32)
    attended = combine(q, suffix_keys, suffix_values, suffix_len.reshape(local, 1), parts)

    weight_uv = lax.ppermute(weight_u, "v", partner(2, 1))

    own_rows = replicate(attended).reshape(-1, HEADS * HD)
    place = jnp.stack([lax.axis_index("c"), lax.axis_index(Y)]).astype(jnp.int32)
    terms = project(
        place, [own_rows, swap(own_rows)], [out_weight, weight_v, weight_u, weight_uv]
    )

    rows, cols = terms.shape[3:]
    arrived = lax.all_to_all(
        terms.reshape(32, 2 * rows, cols), Y + HEAD, 0, 0, tiled=True
    ).reshape(4, 8, 2, 2, local, cols)
    summed = jnp.sum(arrived.astype(jnp.float32), axis=1).astype(jnp.bfloat16)
    return jnp.transpose(summed, (2, 0, 1, 3, 4)).reshape(2, 8 * local, cols)


def solution(mesh):
    split_mesh = Mesh(mesh.devices.reshape(8, 2, 2, 2, 4, 2), SEQ + HEAD)
    in_specs = (
        P(None, SEQ, HEAD),
        P(SEQ + HEAD, None),
        P(SEQ + HEAD, None),
        P(SEQ, None, HEAD),
        P(SEQ, None, HEAD),
        P(None, SEQ, HEAD),
        P(None, SEQ, HEAD),
        P(SEQ),
        P(HEAD, SEQ),
    )
    out_specs = P(None, HEAD, SEQ)
    return jax.shard_map(
        per_device, mesh=split_mesh, in_specs=in_specs, out_specs=out_specs, check_vma=False
    )
```

```python
import functools
import math

import jax
import jax.numpy as jnp
from jax import lax
from jax.experimental import pallas as pl
from jax.experimental.pallas import tpu as pltpu
from jax.sharding import Mesh
from jax.sharding import PartitionSpec as P

HD = 128
SUF = 2
HEADS = 16
LOG2_SCALE = HD ** -0.5 * math.log2(math.e)
Y = ("u", "v")
HEAD = ("x", "w")
SEQ = ("z", "u", "v", "c")
CHUNK = 8
VMEM_BYTES = 48 * 1024 * 1024


def shift(size, step):
    return [(index, (index + step) % size) for index in range(size)]


def partner(size, bits):
    return [(index, index ^ bits) for index in range(size)]


def ring(value):
    blocks = {0: value}
    up = value
    down = value
    for step in range(1, 5):
        up = lax.ppermute(up, "z", shift(8, 1))
        blocks[-step] = up
        if step < 4:
            down = lax.ppermute(down, "z", shift(8, -1))
            blocks[step] = down
        yield blocks


def swap(value):
    return lax.ppermute(value, "c", partner(2, 1))


def after(value, *others, space=pl.ANY):
    def nothing(*refs):
        pass

    return pl.pallas_call(
        nothing,
        out_shape=jax.ShapeDtypeStruct(value.shape, value.dtype),
        in_specs=[pl.BlockSpec(memory_space=space)] + [pl.BlockSpec(memory_space=pl.ANY)] * len(others),
        out_specs=pl.BlockSpec(memory_space=space),
        input_output_aliases={0: 0},
        name="after",
    )(value, *others)


def attention_kernel(q_ref, *refs):
    out_ref = refs[-1]
    rows = q_ref.shape[0]
    half = refs[0].shape[1] // 2
    q = jnp.concatenate([q_ref[:, g * HD : (g + 1) * HD] for g in range(HEADS)], axis=0)
    top = None
    acc = None
    for ref in refs[:-1]:
        for start in range(0, ref.shape[0], CHUNK):
            span = slice(start, start + CHUNK)
            keys = ref[span, :half, :].reshape(-1, HD)
            block = ref[span, half:, :].reshape(-1, HD)
            values = jnp.concatenate([block, jnp.ones_like(block)], axis=1)
            scores = lax.dot_general(
                q, keys, (((1,), (1,)), ((), ())), preferred_element_type=jnp.float32
            )
            highest = scores.max(axis=1, keepdims=True)
            if top is not None:
                highest = jnp.maximum(top, highest)
            weights = jnp.exp2((scores - highest) * LOG2_SCALE).astype(jnp.bfloat16)
            term = jnp.dot(weights, values, preferred_element_type=jnp.float32)
            acc = term if acc is None else acc * jnp.exp2((top - highest) * LOG2_SCALE) + term
            top = highest
    total = acc[:, HD : HD + 1]
    mean = acc[:, :HD] / total
    level = top * LOG2_SCALE + jnp.log2(total)
    first = level.astype(jnp.bfloat16).astype(jnp.float32)
    rest = level - first
    second = rest.astype(jnp.bfloat16).astype(jnp.float32)
    third = rest - second
    lane = lax.broadcasted_iota(jnp.int32, (rows, HD), 1)
    pieces = jnp.zeros((rows, HD), jnp.float32)
    for g in range(HEADS):
        span = slice(g * rows, (g + 1) * rows)
        out_ref[:, g * HD : (g + 1) * HD] = mean[span].astype(jnp.bfloat16)
        for place, piece in enumerate((first, second, third)):
            pieces = jnp.where(lane == place * HEADS + g, piece[span], pieces)
    out_ref[:, HEADS * HD :] = pieces.astype(jnp.bfloat16)


def attend(q, blocks):
    rows = q.shape[0]
    return pl.pallas_call(
        attention_kernel,
        out_shape=jax.ShapeDtypeStruct((rows, HEADS * HD + HD), jnp.bfloat16),
        compiler_params=pltpu.CompilerParams(vmem_limit_bytes=VMEM_BYTES),
        name="attend",
    )(q, *blocks)


def combine_kernel(q_ref, k_ref, v_ref, len_ref, m0_ref, m1_ref, m2_ref, m3_ref, out_ref):
    rows = q_ref.shape[0]
    local = rows // 2
    width = HEADS * HD
    parts = (m0_ref, m1_ref, m2_ref, m3_ref)
    lane = lax.broadcasted_iota(jnp.int32, (rows, HD), 1)
    step_one = lax.broadcasted_iota(jnp.int32, (rows, 1), 0) >= local
    used = jnp.concatenate([len_ref[...], len_ref[...]], axis=0)
    valid = (used > 0, used > 1, used >= 0, step_one)
    suffix_values = []
    logits = []
    for j in range(4):
        key = jnp.concatenate([k_ref[j], k_ref[j]], axis=0)
        suffix_values.append(jnp.concatenate([v_ref[j], v_ref[j]], axis=0))
        row = jnp.full((rows, HD), -1e30, jnp.float32)
        for g in range(HEADS):
            q = q_ref[:, g * HD : (g + 1) * HD].astype(jnp.float32)
            dot = jnp.sum(q * key, axis=1, keepdims=True) * LOG2_SCALE
            row = jnp.where(lane == g, dot, row)
        logits.append(jnp.where(valid[j], row, jnp.float32(-1e30)))
    levels = []
    for ref in parts:
        tail = ref[:, width:].astype(jnp.float32)
        level = tail + pltpu.roll(tail, HD - HEADS, 1) + pltpu.roll(tail, HD - 2 * HEADS, 1)
        levels.append(level)
    top = functools.reduce(jnp.maximum, levels + logits)
    factors = [jnp.exp2(level - top) for level in levels]
    weights = [
        jnp.where(valid[j], jnp.exp2(logits[j] - top), jnp.float32(0.0)) for j in range(4)
    ]
    total = functools.reduce(jnp.add, factors + weights)
    scale = 1.0 / total
    factors = [f * scale for f in factors]
    weights = [w * scale for w in weights]
    for g in range(HEADS):
        cols = slice(g * HD, (g + 1) * HD)
        acc = jnp.zeros((rows, HD), jnp.float32)
        for ref, f in zip(parts, factors):
            acc = acc + f[:, g : g + 1] * ref[:, cols].astype(jnp.float32)
        for j in range(4):
            acc = acc + weights[j][:, g : g + 1] * suffix_values[j]
        merged = acc.astype(jnp.bfloat16)
        for copy in range(out_ref.shape[0]):
            out_ref[copy, :, cols] = merged


def combine(q, keys, values, lens, parts):
    return pl.pallas_call(
        combine_kernel,
        out_shape=jax.ShapeDtypeStruct((8,) + q.shape, jnp.bfloat16),
        compiler_params=pltpu.CompilerParams(vmem_limit_bytes=VMEM_BYTES),
        name="combine",
    )(q, keys, values, lens, *parts)


def project_kernel(place_ref, own_ref, other_ref, *refs):
    weights, out_ref = refs[:4], refs[4]
    rows = out_ref.shape[3]
    core, me = place_ref[0], place_ref[1]
    for index, weight in enumerate(weights):
        column = lax.bitwise_xor(me, index)
        for side, rows_ref in enumerate((own_ref, other_ref)):
            terms = jnp.dot(rows_ref[...], weight[...], preferred_element_type=jnp.float32)
            terms = terms.astype(jnp.bfloat16)
            which = lax.bitwise_xor(core, side)
            for z in range(8):
                out_ref[column, z, which] = terms[z * rows : (z + 1) * rows]


def project(place, blocks, weights):
    rows = blocks[0].shape[0] // 8
    cols = weights[0].shape[1]
    whole = list(blocks) + list(weights)
    return pl.pallas_call(
        project_kernel,
        out_shape=jax.ShapeDtypeStruct((4, 8, 2, rows, cols), jnp.bfloat16),
        in_specs=[pl.BlockSpec(memory_space=pltpu.SMEM)]
        + [pl.BlockSpec(memory_space=pltpu.VMEM)] * len(whole),
        compiler_params=pltpu.CompilerParams(vmem_limit_bytes=VMEM_BYTES),
        name="project",
    )(place, *whole)


def per_device(
    queries,
    prefix_keys,
    prefix_values,
    cache_keys,
    cache_values,
    new_keys,
    new_values,
    suffix_len,
    out_weight,
):
    local = queries.shape[1]
    count = prefix_keys.shape[0]
    q = queries.reshape(2 * local, HEADS * HD)

    q_parts = [q] + [lax.ppermute(q, Y, partner(4, k)) for k in (1, 2, 3)]

    split = [
        jnp.swapaxes(rows.reshape(count, 8, HD), 0, 1) for rows in (prefix_keys, prefix_values)
    ]
    own = lax.all_to_all(jnp.concatenate(split, axis=1), HEAD, 0, 0, tiled=True)
    weight_u = lax.ppermute(out_weight, "u", partner(2, 1))
    weight_v = lax.ppermute(out_weight, "v", partner(2, 1))
    held = []
    for step, blocks in enumerate(ring(own), 1):
        if step == 2:
            near = jnp.concatenate([blocks[offset] for offset in (0, -1, 1, -2, 2)], axis=0)
            held += [near, swap(near)]
        if step == 4:
            last = after(blocks[-4], weight_u, weight_v)
            far = jnp.concatenate([blocks[-3], blocks[3], last], axis=0)
            held += [far, swap(far)]

    parts = [None] * 4
    for k in (2, 3, 1, 0):
        message = attend(q_parts[k], held)
        parts[k] = message if k == 0 else lax.ppermute(message, Y, partner(4, k))

    suffix_keys = jnp.stack(
        [cache_keys[:, 0], cache_keys[:, 1], new_keys[0], new_keys[1]], axis=0
    ).astype(jnp.float32)
    suffix_values = jnp.stack(
        [cache_values[:, 0], cache_values[:, 1], new_values[0], new_values[1]], axis=0
    ).astype(jnp.float32)
    attended = combine(q, suffix_keys, suffix_values, suffix_len.reshape(local, 1), parts)

    weight_uv = lax.ppermute(weight_u, "v", partner(2, 1))

    own_rows = lax.all_to_all(attended, "z", 0, 0, tiled=True).reshape(-1, HEADS * HD)
    place = jnp.stack([lax.axis_index("c"), lax.axis_index(Y)]).astype(jnp.int32)
    terms = project(
        place, [own_rows, swap(own_rows)], [out_weight, weight_v, weight_u, weight_uv]
    )

    rows, cols = terms.shape[3:]
    arrived = lax.all_to_all(
        terms.reshape(32, 2 * rows, cols), Y + HEAD, 0, 0, tiled=True
    ).reshape(4, 8, 2, 2, local, cols)
    summed = jnp.sum(arrived.astype(jnp.float32), axis=1).astype(jnp.bfloat16)
    return jnp.transpose(summed, (2, 0, 1, 3, 4)).reshape(2, 8 * local, cols)


def solution(mesh):
    split_mesh = Mesh(mesh.devices.reshape(8, 2, 2, 2, 4, 2), SEQ + HEAD)
    in_specs = (
        P(None, SEQ, HEAD),
        P(SEQ + HEAD, None),
        P(SEQ + HEAD, None),
        P(SEQ, None, HEAD),
        P(SEQ, None, HEAD),
        P(None, SEQ, HEAD),
        P(None, SEQ, HEAD),
        P(SEQ),
        P(HEAD, SEQ),
    )
    out_specs = P(None, HEAD, SEQ)
    return jax.shard_map(
        per_device, mesh=split_mesh, in_specs=in_specs, out_specs=out_specs, check_vma=False
    )
```
